512 devices in a mesh: dp: 16 (over y, x_hi), expert: 32 (over z, x_lo, core).
Axes of the slice: x: 4 (x_hi: 2, x_lo: 2; x = x_hi * 2 + x_lo), y: 8, z: 8, core: 2. Of those that a mesh axis runs over, the one named last changes fastest.
Arguments:
- acts: bfloat16 [32, 2048, 2560], P('expert', 'dp'), may hold values from -6 to 6
- out_grads: bfloat16 [32, 2048, 768], P('expert', 'dp'), may hold values from -1 to 1
- next_tokens: bfloat16 [32, 2048, 2560], P('expert', 'dp'), may hold values from -6 to 6
- master: float32 [32, 2560, 768], P('expert', 'dp'), may hold values from -0.125 to 0.125
- first_moment: float32 [32, 2560, 768], P('expert', 'dp'), may hold values from -6 to 6
- second_moment: float32 [32, 2560, 768], P('expert', 'dp'), may hold values from 0.5 to 20
- counts: int32 [16, 160], P('dp'), may hold values from 32 to 128
- selected: int32 [32], replicated, may hold values from 0 to 159
- old_place: int32 [32], replicated, may hold values from 0 to 31, each once
- new_place: int32 [32], replicated, may hold values from 0 to 31, each once
Outputs:
- new_master: float32 [32, 2560, 768], P('expert', 'dp')
- new_first: float32 [32, 2560, 768], P('expert', 'dp')
- new_second: float32 [32, 2560, 768], P('expert', 'dp')
- forward: bfloat16 [32, 2048, 768], P('expert', 'dp')
The draws below stay inside these ranges and needn't reach their ends.
Inputs may be any that keep to these rules, and one draw needn't show every extreme that they name: `old_place`: each holder index appears once. `new_place`: each holder index appears once.
All inputs are finite; a program needn't handle non-finite values.
Results may differ from the reference program's by a relative error of at most 0.012.
Values may be sent and summed in bfloat16 or wider, within the bound.
A program may use at most 64 MiB of HBM per device.

```python
import math
import jax
import jax.numpy as jnp
from jax import lax

D = 2560
FF = 768
EXPERTS = 160
TOK_DEV = 128
SLOTS = 32
TOKENS = 2048
N_DP = 16


def plant(drawn, rng, smallest, high):
    place = [jax.random.randint(jax.random.fold_in(rng, axis), (), 0, length) for axis, length in enumerate(drawn.shape)]
    longest = drawn.shape.index(max(drawn.shape))
    neighbour = place[:longest] + [(place[longest] + 1) % drawn.shape[longest]] + place[longest + 1:]
    return drawn.at[tuple(place)].set(smallest).at[tuple(neighbour)].set(high)


def block_scale(key, extent, pieces, least, top_value):
    def one(axis_at, shards_of):
        heights = jax.random.uniform(jax.random.fold_in(jax.random.fold_in(key, 6), axis_at), (shards_of,), jnp.float32, least / len(pieces), top_value / len(pieces))
        return jnp.repeat(jnp.exp(heights), extent[axis_at] // shards_of).reshape((-1,) + (1,) * (len(extent) - axis_at - 1))

    level = one(*pieces[0])
    for cut in pieces[1:]:
        level = level * one(*cut)
    return level


def centred(own_key, dims, spread, limit, cuts=(), kind=jnp.bfloat16):
    loudness = block_scale(own_key, dims, cuts, -0.22, 0.18) if cuts else 1.0
    values = jax.random.normal(own_key, dims, jnp.float32) * spread * loudness
    return jnp.minimum(jnp.maximum(values, -limit), limit).astype(kind)


def setup_inputs(seed: int = 0) -> dict:
    splits = jax.random.split(jax.random.key(seed), 11)
    return {
        "acts": centred(splits[0], (SLOTS, TOKENS, D), 1.0, 6.0, ((0, 32), (1, 16))),
        "out_grads": centred(splits[1], (SLOTS, TOKENS, FF), (3.0 / TOKENS ** 0.5), 1.0, ((0, 32), (1, 16))),
        "next_tokens": centred(splits[2], (SLOTS, TOKENS, D), 1.0, 6.0, ((0, 32), (1, 16))),
        "master": centred(splits[3], (SLOTS, D, FF), D ** -0.5, 0.125, ((0, 32), (1, 16)), jnp.float32),
        "first_moment": centred(splits[4], (SLOTS, D, FF), 1.0, 6.0, ((0, 32), (1, 16)), jnp.float32),
        "second_moment": jnp.clip(jnp.exp(math.log(20.0) - 3.6888795 * jax.random.uniform(splits[5], (SLOTS, D, FF), jnp.float32) ** block_scale(splits[5], (SLOTS, D, FF), ((0, 32), (1, 16)), -0.2, 0.2)), 0.5, 20.0),
        "counts": plant(jax.random.randint(splits[6], (N_DP, EXPERTS), TOK_DEV // 4, TOK_DEV + 1), jax.random.fold_in(splits[6], 1), TOK_DEV // 4, TOK_DEV).astype(jnp.int32),
        "selected": plant(jax.random.randint(splits[7], (SLOTS,), 0, EXPERTS), jax.random.fold_in(splits[7], 1), 0, EXPERTS - 1).astype(jnp.int32),
        "old_place": jax.random.permutation(splits[8], SLOTS).astype(jnp.int32),
        "new_place": jax.random.permutation(splits[9], SLOTS).astype(jnp.int32),
    }


beta_first = 0.9
beta_second = 0.95
bias_first = 1.0 - 0.9 ** 10
bias_second = 1.0 - 0.95 ** 10
learn_rate = 0.01
decay_rate = 0.1
epsilon = 1e-08

def adamw(weights, moment_one, moment_two, gradient):
    moment_one = beta_first * moment_one + (1.0 - beta_first) * gradient
    moment_two = beta_second * moment_two + (1.0 - beta_second) * gradient * gradient
    update = moment_one / bias_first / (jnp.sqrt(moment_two / bias_second) + epsilon) + decay_rate * weights
    return (weights - learn_rate * update, moment_one, moment_two)

def reference(acts, out_grads, next_tokens, master, first_moment, second_moment, counts, selected, old_place, new_place):
    slots = jnp.arange(SLOTS, dtype=jnp.int32)
    holder = lax.optimization_barrier(jnp.sum(jnp.where(old_place[None, :] == slots[:, None], slots[None, :], 0), axis=1)).astype(jnp.int32)
    expert_of = selected[holder]
    routed = jnp.take(counts, expert_of, axis=1).T

    def gradient_of(packed):
        tokens_in, grads_in, routed_in = packed
        live = jnp.arange(TOK_DEV, dtype=jnp.int32)[None, :] < routed_in[:, None]
        grads_in = grads_in.reshape(N_DP, TOK_DEV, FF)
        masked = jnp.where(live[:, :, None], grads_in, jnp.zeros_like(grads_in))
        blocks = jnp.einsum('stk,stf->skf', tokens_in.reshape(N_DP, TOK_DEV, D).astype(jnp.float32), masked.astype(jnp.float32))
        rounded = lax.optimization_barrier(blocks.astype(jnp.bfloat16))
        return lax.optimization_barrier(jnp.sum(rounded.astype(jnp.float32), axis=0))
    gradients = lax.map(gradient_of, (acts, out_grads, routed))
    weights, moment_one, moment_two = adamw(master, first_moment, second_moment, gradients)
    inverse = lax.optimization_barrier(jnp.sum(jnp.where(new_place[None, :] == slots[:, None], slots[None, :], 0), axis=1)).astype(jnp.int32)
    source = old_place[inverse]
    weights = jnp.take(weights, source, axis=0)
    moment_one = jnp.take(moment_one, source, axis=0)
    moment_two = jnp.take(moment_two, source, axis=0)
    lowered = weights.astype(jnp.bfloat16)

    def forward_of(packed):
        tokens_in, weight_in = packed
        return jnp.dot(tokens_in, weight_in, preferred_element_type=jnp.float32).astype(jnp.bfloat16)
    forward = lax.map(forward_of, (next_tokens, lowered))
    return (weights, moment_one, moment_two, forward)
```

```python
import jax
import jax.numpy as jnp
from jax import lax
from jax.experimental import pallas as pl
from jax.experimental.pallas import tpu as pltpu
from jax.sharding import PartitionSpec as P

MESH = pl.DeviceIdType.MESH

beta_first = 0.9
beta_second = 0.95
bias_first = 1.0 - 0.9**10
bias_second = 1.0 - 0.95**10
learn_rate = 0.01
decay_rate = 0.1
epsilon = 1e-08

RING = 8
ROWS = 160
WIDE = 384
TOK = 128
HOLD = 32
RELAYS = 30
F32 = jnp.float32
BF16 = jnp.bfloat16
CHAINS = ((0, 1, 4), (1, -1, 4), (1, 1, 3), (0, -1, 3))


def adamw(weights, moment_one, moment_two, gradient):
    moment_one = beta_first * moment_one + (1.0 - beta_first) * gradient
    moment_two = beta_second * moment_two + (1.0 - beta_second) * gradient * gradient
    update = (
        moment_one / bias_first / (jnp.sqrt(moment_two / bias_second) + epsilon)
        + decay_rate * weights
    )
    return (weights - learn_rate * update, moment_one, moment_two)


def kernel(
    counts, selected, old_place, new_place,
    acts, grads, tokens, master, first, second,
    out_w, out_m, out_v, out_f,
    order, at, nt, at_in, nt_in, ntx, g_own, g_in, term,
    rs_out, rs_in, stage_w, relay_a, relay_b, sorted_w, stage_m, relay_m, sorted_m, new_w, new_m,
    gathered, f_out, f_in, f_own,
    x_send, x_recv, rs_send, rs_recv, ag_send, ag_recv, p_send, p_recv, f_send, f_recv,
):
    dp, me = lax.axis_index("dp"), lax.axis_index("expert")
    relay_w = (relay_a, relay_b)
    y, par = dp // 2, dp % 2
    other = 1 - par
    partner = (y * 2 + other, me)
    up = (((y + 1) % RING) * 2 + par, me)
    down = (((y + RING - 1) % RING) * 2 + par, me)

    barrier = pltpu.get_barrier_semaphore()
    for peer in (partner, up, down):
        pl.semaphore_signal(barrier, inc=1, device_id=peer, device_id_type=MESH)

    def greet(j, c):
        pl.semaphore_signal(
            barrier, inc=1, device_id=(dp, (me + j) % HOLD), device_id_type=MESH
        )
        return c

    lax.fori_loop(1, HOLD, greet, 0)

    def push(src, dst, send, recv, to):
        copy = pltpu.make_async_remote_copy(
            src_ref=src, dst_ref=dst, send_sem=send, recv_sem=recv,
            device_id=to, device_id_type=MESH,
        )
        copy.start()

    def got(ref, sem):
        pltpu.make_async_copy(ref, ref, sem).wait()

    def all_but(ref, sems, count, mine):
        def go(n, c):
            @pl.when(n != mine)
            def _():
                got(ref.at[n], sems.at[n])

            return c

        lax.fori_loop(0, count, go, 0)

    def find(i, c):
        return c + jnp.where(old_place[i] == me, selected[i], 0)

    expert_id = lax.fori_loop(0, HOLD, find, jnp.int32(0))
    routed = counts[0, expert_id]
    live = lax.broadcasted_iota(jnp.int32, (TOK, 768), 0) < routed
    value = grads[...]
    g_own[...] = jnp.where(live, value, jnp.zeros_like(value))

    def turned(src, dst):
        for i in range(20):
            tile = src[:, i * 128 : (i + 1) * 128].T
            for m in range(4):
                row = i * 128 + m * 32
                block, at_row = row // ROWS, row % ROWS
                dst[block % 2, block // 2, at_row : at_row + 32, :] = tile[m * 32 : (m + 1) * 32]

    turned(acts, at)
    pl.semaphore_wait(barrier, 3 + HOLD - 1)

    push(g_own, g_in, x_send.at[8], x_recv.at[8], partner)
    for k in (4, 3, 5, 2, 6, 1, 7, 0):
        t = (y + k) % RING
        push(at.at[other, t], at_in.at[k], x_send.at[k], x_recv.at[k], partner)
    turned(tokens, nt)
    push(nt.at[other], nt_in, x_send.at[9], x_recv.at[9], partner)

    def place(d, c):
        def look(i, c):
            return c + jnp.where(new_place[i] == d, old_place[i], 0)

        order[d] = lax.fori_loop(0, HOLD, look, jnp.int32(0), unroll=True)
        return c

    lax.fori_loop(0, HOLD, place, 0)

    def contribution(k, h):
        t = (y + k) % RING
        cols = slice(h * WIDE, (h + 1) * WIDE)
        return jnp.dot(at[par, t], g_own[:, cols], preferred_element_type=F32) + jnp.dot(
            at_in[k], g_in[:, cols], preferred_element_type=F32
        )

    got(g_in, x_recv.at[8])
    arrived = set()
    for s in range(4):
        for c, (h, way, hops) in enumerate(CHAINS):
            if s >= hops:
                continue
            k = (way * (hops - s)) % RING
            if k not in arrived:
                arrived.add(k)
                got(at_in.at[k], x_recv.at[k])
            own = contribution(k, h)
            if s == 0:
                rs_out[c, s] = own.astype(BF16)
            else:
                term[...] = own
                got(rs_in.at[c, s - 1], rs_recv.at[c, s - 1])
                rs_out[c, s] = (rs_in[c, s - 1].astype(F32) + term[...]).astype(BF16)
            push(
                rs_out.at[c, s], rs_in.at[c, s], rs_send.at[c, s], rs_recv.at[c, s],
                up if way == 1 else down,
            )
    got(at_in.at[0], x_recv.at[0])

    def one_phase_out(stage, relay, send, recv, first_relay):
        def go(n, c):
            j = n + first_relay

            @pl.when(j != me)
            def _():
                push(stage.at[n], relay.at[me], send.at[n], recv.at[me], (dp, j))

            return c

        lax.fori_loop(0, RELAYS, go, 0)

    for h in range(2):
        term[...] = contribution(0, h)
        for c, (half, way, hops) in enumerate(CHAINS):
            if half == h:
                got(rs_in.at[c, hops - 1], rs_recv.at[c, hops - 1])
        ends = [(c, hops - 1) for c, (half, _, hops) in enumerate(CHAINS) if half == h]
        for k in range(10):
            for q in range(3):
                rows = slice(16 * k, 16 * k + 16)
                local = slice(128 * q, 128 * q + 128)
                cols = slice(h * WIDE + 128 * q, h * WIDE + 128 * q + 128)
                total = term[rows, local]
                for c, s in ends:
                    total = total + rs_in[c, s, rows, local].astype(F32)
                w, m, v = adamw(master[rows, cols], first[rows, cols], second[rows, cols], total)
                p = 3 * k + q
                stage_w[h, p] = w.astype(BF16)
                stage_m[p, 2 * h] = m.astype(BF16)
                stage_m[p, 2 * h + 1] = v.astype(BF16)
        one_phase_out(stage_w.at[h], relay_w[h], p_send.at[0, h], p_recv.at[0, h], 0)

        @pl.when(me < RELAYS)
        def _():
            relay_w[h][me] = stage_w[h, me]

    one_phase_out(stage_m, relay_m, p_send.at[0, 2], p_recv.at[0, 2], 2)

    @pl.when(me >= 2)
    def _():
        relay_m[me] = stage_m[me - 2]

    def two_phase_out(relay, ordered, final, send, recv, first_relay):
        slot = me - first_relay

        @pl.when((me >= first_relay) & (me < first_relay + RELAYS))
        def _():
            all_but(relay, recv[0], HOLD, me)

            def go(d, c):
                ordered[d] = relay[order[d]]

                @pl.when(d != me)
                def _():
                    push(ordered.at[d], final.at[slot], send[1].at[d], recv[1].at[slot], (dp, d))

                return c

            lax.fori_loop(0, HOLD, go, 0)
            final[slot] = ordered[me]

    def two_phase_in(final, recv, first_relay):
        all_but(final, recv, RELAYS, me - first_relay)

    for h in range(2):
        two_phase_out(
            relay_w[h], sorted_w.at[h], new_w.at[h],
            (p_send.at[0, h], p_send.at[1, h]), (p_recv.at[0, h], p_recv.at[1, h]), 0,
        )
    for h in range(2):
        two_phase_in(new_w.at[h], p_recv.at[1, h], 0)
        for p in range(RELAYS):
            k, q = p // 3, p % 3
            gathered[h, y, 16 * k : 16 * k + 16, 128 * q : 128 * q + 128] = new_w[h, p]
        for c, (half, way, hops) in enumerate(CHAINS):
            if half == h:
                mine = gathered.at[h, y]
                push(mine, mine, ag_send.at[c, 0], ag_recv.at[c, 0], up if way == 1 else down)
    two_phase_out(
        relay_m, sorted_m, new_m,
        (p_send.at[0, 2], p_send.at[1, 2]), (p_recv.at[0, 2], p_recv.at[1, 2]), 2,
    )
    for p in range(RELAYS):
        k, q = p // 3, p % 3
        for h in range(2):
            cols = slice(h * WIDE + 128 * q, h * WIDE + 128 * q + 128)
            out_w[16 * k : 16 * k + 16, cols] = new_w[h, p].astype(F32)

    got(nt_in, x_recv.at[9])
    for i in range(10):
        ntx[0:128, 128 * i : 128 * i + 128] = jnp.concatenate(
            [nt_in[(128 * i + 32 * m) // ROWS, (128 * i + 32 * m) % ROWS : (128 * i + 32 * m) % ROWS + 32] for m in range(4)], axis=0
        ).T
        ntx[128:256, 128 * i : 128 * i + 128] = jnp.concatenate(
            [nt[par, (128 * i + 32 * m) // ROWS, (128 * i + 32 * m) % ROWS : (128 * i + 32 * m) % ROWS + 32] for m in range(4)], axis=0
        ).T

    for s in range(1, 5):
        for c, (h, way, hops) in enumerate(CHAINS):
            if s > hops:
                continue
            block = gathered.at[h, (y - way * s) % RING]
            got(block, ag_recv.at[c, s - 1])
            if s < hops:
                push(block, block, ag_send.at[c, s], ag_recv.at[c, s], up if way == 1 else down)

    for h in range(2):
        whole = gathered[h].reshape(RING * ROWS, WIDE)
        f_out[h] = jnp.dot(ntx[0:128], whole, preferred_element_type=F32).astype(BF16)
        push(f_out.at[h], f_in.at[h], f_send.at[h], f_recv.at[h], partner)
    for h in range(2):
        whole = gathered[h].reshape(RING * ROWS, WIDE)
        f_own[h] = jnp.dot(ntx[128:256], whole, preferred_element_type=F32)

    two_phase_in(new_m, p_recv.at[1, 2], 2)
    for p in range(RELAYS):
        k, q = p // 3, p % 3
        for h in range(2):
            cols = slice(h * WIDE + 128 * q, h * WIDE + 128 * q + 128)
            out_m[16 * k : 16 * k + 16, cols] = new_m[p, 2 * h].astype(F32)
            out_v[16 * k : 16 * k + 16, cols] = new_m[p, 2 * h + 1].astype(F32)

    for h in range(2):
        got(f_in.at[h], f_recv.at[h])
        out_f[:, h * WIDE : (h + 1) * WIDE] = (f_own[h] + f_in[h].astype(F32)).astype(BF16)

    for k in range(8):
        got(at_in.at[0], x_send.at[k])
    got(g_own, x_send.at[8])
    got(nt_in, x_send.at[9])
    for c, (h, way, hops) in enumerate(CHAINS):
        for s in range(hops):
            got(rs_out.at[c, s], rs_send.at[c, s])
            got(gathered.at[0, 0], ag_send.at[c, s])
    for h in range(2):
        got(f_out.at[h], f_send.at[h])

    def sent(stage, relay, one, two, first_relay):
        all_but(stage, one, RELAYS, me - first_relay)

        @pl.when((me >= first_relay) & (me < first_relay + RELAYS))
        def _():
            all_but(relay, two, HOLD, me)

    for h in range(2):
        sent(stage_w.at[h], relay_w[h], p_send.at[0, h], p_send.at[1, h], 0)
    sent(stage_m, relay_m, p_send.at[0, 2], p_send.at[1, 2], 2)


def body(
    acts, out_grads, next_tokens, master, first_moment, second_moment,
    counts, selected, old_place, new_place,
):
    vmem = pl.BlockSpec(memory_space=pltpu.VMEM)
    smem = pl.BlockSpec(memory_space=pltpu.SMEM)
    state = jax.ShapeDtypeStruct((ROWS, 768), F32)
    w, m, v, f = pl.pallas_call(
        kernel,
        out_shape=(state, state, state, jax.ShapeDtypeStruct((TOK, 768), BF16)),
        in_specs=[smem] * 4 + [vmem] * 6,
        out_specs=(vmem,) * 4,
        scratch_shapes=[
            pltpu.SMEM((HOLD,), jnp.int32),
            pltpu.VMEM((2, RING, ROWS, TOK), BF16),
            pltpu.VMEM((2, RING, ROWS, TOK), BF16),
            pltpu.VMEM((RING, ROWS, TOK), BF16),
            pltpu.VMEM((RING, ROWS, TOK), BF16),
            pltpu.VMEM((2 * TOK, RING * ROWS), BF16),
            pltpu.VMEM((TOK, 768), BF16),
            pltpu.VMEM((TOK, 768), BF16),
            pltpu.VMEM((ROWS, WIDE), F32),
            pltpu.VMEM((4, 4, ROWS, WIDE), BF16),
            pltpu.VMEM((4, 4, ROWS, WIDE), BF16),
            pltpu.VMEM((2, RELAYS, 16, 128), BF16),
            pltpu.VMEM((HOLD, 16, 128), BF16),
            pltpu.VMEM((HOLD, 16, 128), BF16),
            pltpu.VMEM((2, HOLD, 16, 128), BF16),
            pltpu.VMEM((RELAYS, 4, 16, 128), BF16),
            pltpu.VMEM((HOLD, 4, 16, 128), BF16),
            pltpu.VMEM((HOLD, 4, 16, 128), BF16),
            pltpu.VMEM((2, RELAYS, 16, 128), BF16),
            pltpu.VMEM((RELAYS, 4, 16, 128), BF16),
            pltpu.VMEM((2, RING, ROWS, WIDE), BF16),
            pltpu.VMEM((2, TOK, WIDE), BF16),
            pltpu.VMEM((2, TOK, WIDE), BF16),
            pltpu.VMEM((2, TOK, WIDE), F32),
            pltpu.SemaphoreType.DMA((10,)),
            pltpu.SemaphoreType.DMA((10,)),
            pltpu.SemaphoreType.DMA((4, 4)),
            pltpu.SemaphoreType.DMA((4, 4)),
            pltpu.SemaphoreType.DMA((4, 4)),
            pltpu.SemaphoreType.DMA((4, 4)),
            pltpu.SemaphoreType.DMA((2, 3, HOLD)),
            pltpu.SemaphoreType.DMA((2, 3, HOLD)),
            pltpu.SemaphoreType.DMA((2,)),
            pltpu.SemaphoreType.DMA((2,)),
        ],
        compiler_params=pltpu.CompilerParams(
            collective_id=0, has_side_effects=True, vmem_limit_bytes=48 * 2**20
        ),
    )(
        counts, selected, old_place, new_place,
        acts[0], out_grads[0], next_tokens[0], master[0], first_moment[0], second_moment[0],
    )
    return w[None], m[None], v[None], f[None]


def solution(mesh):
    both = P("expert", "dp", None)
    return jax.shard_map(
        body,
        mesh=mesh,
        in_specs=(both,) * 6 + (P("dp", None), P(), P(), P()),
        out_specs=(both,) * 4,
        check_vma=False,
    )
```

```python
import jax
import jax.numpy as jnp
from jax import lax
from jax.experimental import pallas as pl
from jax.experimental.pallas import tpu as pltpu
from jax.sharding import PartitionSpec as P

MESH = pl.DeviceIdType.MESH

beta_first = 0.9
beta_second = 0.95
bias_first = 1.0 - 0.9**10
bias_second = 1.0 - 0.95**10
learn_rate = 0.01
decay_rate = 0.1
epsilon = 1e-08

RING = 8
ROWS = 160
WIDE = 384
TOK = 128
HOLD = 32
RELAYS = 30
F32 = jnp.float32
BF16 = jnp.bfloat16
CHAINS = ((0, 1, 4), (1, -1, 4), (1, 1, 3), (0, -1, 3))


def adamw(weights, moment_one, moment_two, gradient):
    moment_one = beta_first * moment_one + (1.0 - beta_first) * gradient
    moment_two = beta_second * moment_two + (1.0 - beta_second) * gradient * gradient
    update = (
        moment_one / bias_first / (jnp.sqrt(moment_two / bias_second) + epsilon)
        + decay_rate * weights
    )
    return (weights - learn_rate * update, moment_one, moment_two)


def kernel(
    counts_hbm, selected_hbm, old_hbm, new_hbm,
    acts_hbm, grads_hbm, tokens_hbm, master_hbm, first_hbm, second_hbm,
    out_w, out_m, out_v, out_f,
    counts, selected, old_place, new_place, acts, grads, tokens, master, first, second, in_sem,
    order, at, nt, at_in, nt_in, ntx, g_own, g_in, term,
    rs_out, rs_in, stage_w, relay_a, relay_b, sorted_w, stage_m, relay_m, sorted_m, new_w, new_m,
    gathered, f_out, f_in, f_own,
    x_send, x_recv, rs_send, rs_recv, ag_send, ag_recv, p_send, p_recv, f_send, f_recv,
):
    dp, me = lax.axis_index("dp"), lax.axis_index("expert")
    relay_w = (relay_a, relay_b)
    y, par = dp // 2, dp % 2
    other = 1 - par
    partner = (y * 2 + other, me)
    up = (((y + 1) % RING) * 2 + par, me)
    down = (((y + RING - 1) % RING) * 2 + par, me)

    reads = [
        pltpu.make_async_copy(src, dst, in_sem.at[i])
        for i, (src, dst) in enumerate((
            (counts_hbm, counts), (selected_hbm, selected), (old_hbm, old_place),
            (new_hbm, new_place), (acts_hbm, acts), (grads_hbm, grads), (tokens_hbm, tokens),
            (master_hbm, master), (first_hbm, first), (second_hbm, second),
        ))
    ]
    for read in reads:
        read.start()

    barrier = pltpu.get_barrier_semaphore()
    for peer in (partner, up, down):
        pl.semaphore_signal(barrier, inc=1, device_id=peer, device_id_type=MESH)

    def greet(j, c):
        pl.semaphore_signal(
            barrier, inc=1, device_id=(dp, (me + j) % HOLD), device_id_type=MESH
        )
        return c

    lax.fori_loop(1, HOLD, greet, 0)

    def push(src, dst, send, recv, to):
        copy = pltpu.make_async_remote_copy(
            src_ref=src, dst_ref=dst, send_sem=send, recv_sem=recv,
            device_id=to, device_id_type=MESH,
        )
        copy.start()

    def got(ref, sem):
        pltpu.make_async_copy(ref, ref, sem).wait()

    for i in (0, 1, 2, 3, 5):
        reads[i].wait()

    def find(i, c):
        return c + jnp.where(old_place[i] == me, selected[i], 0)

    expert_id = lax.fori_loop(0, HOLD, find, jnp.int32(0))
    routed = counts[0, expert_id]
    live = lax.broadcasted_iota(jnp.int32, (TOK, 768), 0) < routed
    value = grads[...]
    g_own[...] = jnp.where(live, value, jnp.zeros_like(value))

    def turned(src, dst):
        for i in range(20):
            tile = src[:, i * 128 : (i + 1) * 128].T
            for m in range(4):
                row = i * 128 + m * 32
                block, at_row = row // ROWS, row % ROWS
                dst[block % 2, block // 2, at_row : at_row + 32, :] = tile[m * 32 : (m + 1) * 32]

    reads[4].wait()
    turned(acts, at)
    pl.semaphore_wait(barrier, 3 + HOLD - 1)

    push(g_own, g_in, x_send.at[8], x_recv.at[8], partner)
    for k in (4, 3, 5, 2, 6, 1, 7, 0):
        t = (y + k) % RING
        push(at.at[other, t], at_in.at[k], x_send.at[k], x_recv.at[k], partner)
    reads[6].wait()
    turned(tokens, nt)
    push(nt.at[other], nt_in, x_send.at[9], x_recv.at[9], partner)

    def place(d, c):
        def look(i, c):
            return c + jnp.where(new_place[i] == d, old_place[i], 0)

        order[d] = lax.fori_loop(0, HOLD, look, jnp.int32(0), unroll=True)
        return c

    lax.fori_loop(0, HOLD, place, 0)

    def contribution(k, h):
        t = (y + k) % RING
        cols = slice(h * WIDE, (h + 1) * WIDE)
        return jnp.dot(at[par, t], g_own[:, cols], preferred_element_type=F32) + jnp.dot(
            at_in[k], g_in[:, cols], preferred_element_type=F32
        )

    got(g_in, x_recv.at[8])
    arrived = set()
    for s in range(4):
        for c, (h, way, hops) in enumerate(CHAINS):
            if s >= hops:
                continue
            k = (way * (hops - s)) % RING
            if k not in arrived:
                arrived.add(k)
                got(at_in.at[k], x_recv.at[k])
            own = contribution(k, h)
            if s == 0:
                rs_out[c, s] = own.astype(BF16)
            else:
                term[...] = own
                got(rs_in.at[c, s - 1], rs_recv.at[c, s - 1])
                rs_out[c, s] = (rs_in[c, s - 1].astype(F32) + term[...]).astype(BF16)
            push(
                rs_out.at[c, s], rs_in.at[c, s], rs_send.at[c, s], rs_recv.at[c, s],
                up if way == 1 else down,
            )
    got(at_in.at[0], x_recv.at[0])

    def one_phase_out(stage, relay, send, recv, first_relay):
        def go(n, c):
            j = n + first_relay

            @pl.when(j != me)
            def _():
                push(stage.at[n], relay.at[me], send, recv, (dp, j))

            return c

        lax.fori_loop(0, RELAYS, go, 0)

    for i in (7, 8, 9):
        reads[i].wait()
    for h in range(2):
        term[...] = contribution(0, h)
        for c, (half, way, hops) in enumerate(CHAINS):
            if half == h:
                got(rs_in.at[c, hops - 1], rs_recv.at[c, hops - 1])
        ends = [(c, hops - 1) for c, (half, _, hops) in enumerate(CHAINS) if half == h]
        for k in range(10):
            for q in range(3):
                rows = slice(16 * k, 16 * k + 16)
                local = slice(128 * q, 128 * q + 128)
                cols = slice(h * WIDE + 128 * q, h * WIDE + 128 * q + 128)
                total = term[rows, local]
                for c, s in ends:
                    total = total + rs_in[c, s, rows, local].astype(F32)
                w, m, v = adamw(master[rows, cols], first[rows, cols], second[rows, cols], total)
                p = 3 * k + q
                stage_w[h, p] = w.astype(BF16)
                stage_m[p, 2 * h] = m.astype(BF16)
                stage_m[p, 2 * h + 1] = v.astype(BF16)
        one_phase_out(stage_w.at[h], relay_w[h], p_send.at[0, h], p_recv.at[0, h], 0)

        @pl.when(me < RELAYS)
        def _():
            relay_w[h][me] = stage_w[h, me]

    def two_phase_out(relay, ordered, final, send, recv, first_relay):
        slot = me - first_relay

        @pl.when((me >= first_relay) & (me < first_relay + RELAYS))
        def _():
            got(relay.at[pl.ds(0, HOLD - 1)], recv[0])

            def go(d, c):
                ordered[d] = relay[order[d]]

                @pl.when(d != me)
                def _():
                    push(ordered.at[d], final.at[slot], send[1], recv[1], (dp, d))

                return c

            lax.fori_loop(0, HOLD, go, 0)
            final[slot] = ordered[me]

    def two_phase_in(final, recv, first_relay):
        relaying = (me >= first_relay) & (me < first_relay + RELAYS)

        @pl.when(relaying)
        def _():
            got(final.at[pl.ds(0, RELAYS - 1)], recv)

        @pl.when(jnp.logical_not(relaying))
        def _():
            got(final, recv)

    for h in range(2):
        two_phase_out(
            relay_w[h], sorted_w.at[h], new_w.at[h],
            (p_send.at[0, h], p_send.at[1, h]), (p_recv.at[0, h], p_recv.at[1, h]), 0,
        )
    for h in range(2):
        two_phase_in(new_w.at[h], p_recv.at[1, h], 0)
        for p in range(RELAYS):
            k, q = p // 3, p % 3
            gathered[h, y, 16 * k : 16 * k + 16, 128 * q : 128 * q + 128] = new_w[h, p]
        for c, (half, way, hops) in enumerate(CHAINS):
            if half == h:
                mine = gathered.at[h, y]
                push(mine, mine, ag_send.at[c, 0], ag_recv.at[c, 0], up if way == 1 else down)
    one_phase_out(stage_m, relay_m, p_send.at[0, 2], p_recv.at[0, 2], 2)

    @pl.when(me >= 2)
    def _():
        relay_m[me] = stage_m[me - 2]

    for p in range(RELAYS):
        k, q = p // 3, p % 3
        for h in range(2):
            cols = slice(h * WIDE + 128 * q, h * WIDE + 128 * q + 128)
            out_w[16 * k : 16 * k + 16, cols] = new_w[h, p].astype(F32)

    got(nt_in, x_recv.at[9])
    for i in range(10):
        ntx[0:128, 128 * i : 128 * i + 128] = jnp.concatenate(
            [nt_in[(128 * i + 32 * m) // ROWS, (128 * i + 32 * m) % ROWS : (128 * i + 32 * m) % ROWS + 32] for m in range(4)], axis=0
        ).T
        ntx[128:256, 128 * i : 128 * i + 128] = jnp.concatenate(
            [nt[par, (128 * i + 32 * m) // ROWS, (128 * i + 32 * m) % ROWS : (128 * i + 32 * m) % ROWS + 32] for m in range(4)], axis=0
        ).T

    def forward_out(h):
        whole = gathered[h].reshape(RING * ROWS, WIDE)
        f_out[h] = jnp.dot(ntx[0:128], whole, preferred_element_type=F32).astype(BF16)
        push(f_out.at[h], f_in.at[h], f_send.at[h], f_recv.at[h], partner)

    for s in range(1, 5):
        for c, (h, way, hops) in enumerate(CHAINS):
            if s > hops:
                continue
            block = gathered.at[h, (y - way * s) % RING]
            got(block, ag_recv.at[c, s - 1])
            if s < hops:
                push(block, block, ag_send.at[c, s], ag_recv.at[c, s], up if way == 1 else down)
            if s == 4:
                forward_out(h)
        if s == 2:
            two_phase_out(
                relay_m, sorted_m, new_m,
                (p_send.at[0, 2], p_send.at[1, 2]), (p_recv.at[0, 2], p_recv.at[1, 2]), 2,
            )
    for h in range(2):
        whole = gathered[h].reshape(RING * ROWS, WIDE)
        f_own[h] = jnp.dot(ntx[128:256], whole, preferred_element_type=F32)

    two_phase_in(new_m, p_recv.at[1, 2], 2)
    for p in range(RELAYS):
        k, q = p // 3, p % 3
        for h in range(2):
            cols = slice(h * WIDE + 128 * q, h * WIDE + 128 * q + 128)
            out_m[16 * k : 16 * k + 16, cols] = new_m[p, 2 * h].astype(F32)
            out_v[16 * k : 16 * k + 16, cols] = new_m[p, 2 * h + 1].astype(F32)

    for h in range(2):
        got(f_in.at[h], f_recv.at[h])
        out_f[:, h * WIDE : (h + 1) * WIDE] = (f_own[h] + f_in[h].astype(F32)).astype(BF16)

    for k in range(8):
        got(at_in.at[0], x_send.at[k])
    got(g_own, x_send.at[8])
    got(nt_in, x_send.at[9])
    for c, (h, way, hops) in enumerate(CHAINS):
        for s in range(hops):
            got(rs_out.at[c, s], rs_send.at[c, s])
            got(gathered.at[0, 0], ag_send.at[c, s])
    for h in range(2):
        got(f_out.at[h], f_send.at[h])

    def sent(stage, relay, one, two, first_relay):
        relaying = (me >= first_relay) & (me < first_relay + RELAYS)

        @pl.when(relaying)
        def _():
            got(stage.at[pl.ds(0, RELAYS - 1)], one)
            got(relay.at[pl.ds(0, HOLD - 1)], two)

        @pl.when(jnp.logical_not(relaying))
        def _():
            got(stage, one)

    for h in range(2):
        sent(stage_w.at[h], relay_w[h], p_send.at[0, h], p_send.at[1, h], 0)
    sent(stage_m, relay_m, p_send.at[0, 2], p_send.at[1, 2], 2)


def write(w, m, v, f, out_w, out_m, out_v, out_f, w_held, m_held, v_held, f_held, sems):
    held = (w_held, m_held, v_held, f_held)
    reads = [
        pltpu.make_async_copy(src, dst, sems.at[0, i])
        for i, (src, dst) in enumerate(zip((w, m, v, f), held))
    ]
    writes = [
        pltpu.make_async_copy(src, dst, sems.at[1, i])
        for i, (src, dst) in enumerate(zip(held, (out_w, out_m, out_v, out_f)))
    ]
    for copy in reads:
        copy.start()
    for copy, after in zip(reads, writes):
        copy.wait()
        after.start()
    for copy in writes:
        copy.wait()


def body(
    acts, out_grads, next_tokens, master, first_moment, second_moment,
    counts, selected, old_place, new_place,
):
    vmem = pl.BlockSpec(memory_space=pltpu.VMEM)
    anywhere = pl.BlockSpec(memory_space=pl.ANY)
    state = jax.ShapeDtypeStruct((ROWS, 768), F32)
    w, m, v, f = pl.pallas_call(
        kernel,
        out_shape=(state, state, state, jax.ShapeDtypeStruct((TOK, 768), BF16)),
        in_specs=[anywhere] * 10,
        out_specs=(vmem,) * 4,
        scratch_shapes=[
            pltpu.SMEM(counts.shape, jnp.int32),
            pltpu.SMEM((HOLD,), jnp.int32),
            pltpu.SMEM((HOLD,), jnp.int32),
            pltpu.SMEM((HOLD,), jnp.int32),
            pltpu.VMEM((TOK, 2560), BF16),
            pltpu.VMEM((TOK, 768), BF16),
            pltpu.VMEM((TOK, 2560), BF16),
            pltpu.VMEM((ROWS, 768), F32),
            pltpu.VMEM((ROWS, 768), F32),
            pltpu.VMEM((ROWS, 768), F32),
            pltpu.SemaphoreType.DMA((10,)),
            pltpu.SMEM((HOLD,), jnp.int32),
            pltpu.VMEM((2, RING, ROWS, TOK), BF16),
            pltpu.VMEM((2, RING, ROWS, TOK), BF16),
            pltpu.VMEM((RING, ROWS, TOK), BF16),
            pltpu.VMEM((RING, ROWS, TOK), BF16),
            pltpu.VMEM((2 * TOK, RING * ROWS), BF16),
            pltpu.VMEM((TOK, 768), BF16),
            pltpu.VMEM((TOK, 768), BF16),
            pltpu.VMEM((ROWS, WIDE), F32),
            pltpu.VMEM((4, 4, ROWS, WIDE), BF16),
            pltpu.VMEM((4, 4, ROWS, WIDE), BF16),
            pltpu.VMEM((2, RELAYS, 16, 128), BF16),
            pltpu.VMEM((HOLD, 16, 128), BF16),
            pltpu.VMEM((HOLD, 16, 128), BF16),
            pltpu.VMEM((2, HOLD, 16, 128), BF16),
            pltpu.VMEM((RELAYS, 4, 16, 128), BF16),
            pltpu.VMEM((HOLD, 4, 16, 128), BF16),
            pltpu.VMEM((HOLD, 4, 16, 128), BF16),
            pltpu.VMEM((2, RELAYS, 16, 128), BF16),
            pltpu.VMEM((RELAYS, 4, 16, 128), BF16),
            pltpu.VMEM((2, RING, ROWS, WIDE), BF16),
            pltpu.VMEM((2, TOK, WIDE), BF16),
            pltpu.VMEM((2, TOK, WIDE), BF16),
            pltpu.VMEM((2, TOK, WIDE), F32),
            pltpu.SemaphoreType.DMA((10,)),
            pltpu.SemaphoreType.DMA((10,)),
            pltpu.SemaphoreType.DMA((4, 4)),
            pltpu.SemaphoreType.DMA((4, 4)),
            pltpu.SemaphoreType.DMA((4, 4)),
            pltpu.SemaphoreType.DMA((4, 4)),
            pltpu.SemaphoreType.DMA((2, 3)),
            pltpu.SemaphoreType.DMA((2, 3)),
            pltpu.SemaphoreType.DMA((2,)),
            pltpu.SemaphoreType.DMA((2,)),
        ],
        compiler_params=pltpu.CompilerParams(
            collective_id=0, has_side_effects=True, vmem_limit_bytes=60 * 2**20
        ),
    )(
        counts, selected, old_place, new_place,
        acts[0], out_grads[0], next_tokens[0], master[0], first_moment[0], second_moment[0],
    )
    w, m, v, f = pl.pallas_call(
        write,
        out_shape=(state, state, state, jax.ShapeDtypeStruct((TOK, 768), BF16)),
        in_specs=[anywhere] * 4,
        out_specs=(anywhere,) * 4,
        scratch_shapes=[pltpu.VMEM((ROWS, 768), F32)] * 3
        + [pltpu.VMEM((TOK, 768), BF16), pltpu.SemaphoreType.DMA((2, 4))],
        compiler_params=pltpu.CompilerParams(vmem_limit_bytes=60 * 2**20),
    )(w, m, v, f)
    return w[None], m[None], v[None], f[None]


def solution(mesh):
    both = P("expert", "dp", None)
    return jax.shard_map(
        body,
        mesh=mesh,
        in_specs=(both,) * 6 + (P("dp", None), P(), P(), P()),
        out_specs=(both,) * 4,
        check_vma=False,
    )
```

```python
import jax
import jax.numpy as jnp
from jax import lax
from jax.experimental import pallas as pl
from jax.experimental.pallas import tpu as pltpu
from jax.sharding import PartitionSpec as P

MESH = pl.DeviceIdType.MESH

beta_first = 0.9
beta_second = 0.95
bias_first = 1.0 - 0.9**10
bias_second = 1.0 - 0.95**10
learn_rate = 0.01
decay_rate = 0.1
epsilon = 1e-08

RING = 8
ROWS = 160
WIDE = 384
TOK = 128
HOLD = 32
RELAYS = 30
F32 = jnp.float32
BF16 = jnp.bfloat16
CHAINS = ((0, 1, 4), (1, -1, 4), (1, 1, 3), (0, -1, 3))


def adamw(weights, moment_one, moment_two, gradient):
    moment_one = beta_first * moment_one + (1.0 - beta_first) * gradient
    moment_two = beta_second * moment_two + (1.0 - beta_second) * gradient * gradient
    update = (
        moment_one / bias_first / (jnp.sqrt(moment_two / bias_second) + epsilon)
        + decay_rate * weights
    )
    return (weights - learn_rate * update, moment_one, moment_two)


def kernel(
    counts_hbm, selected_hbm, old_hbm, new_hbm,
    acts_hbm, grads_hbm, tokens_hbm, master_hbm, first_hbm, second_hbm,
    out_w, out_m, out_v, out_f,
    counts, selected, old_place, new_place, acts, grads, tokens, master, first, second, in_sem,
    order, at, nt, at_in, nt_in, ntx, g_own, g_in, term,
    rs_out, rs_in, stage_w, relay_a, relay_b, sorted_w, stage_m, relay_m, sorted_m, new_w, new_m,
    gathered, f_out, f_in, f_own,
    x_send, x_recv, rs_send, rs_recv, ag_send, ag_recv, p_send, p_recv, f_send, f_recv,
):
    dp, me = lax.axis_index("dp"), lax.axis_index("expert")
    relay_w = (relay_a, relay_b)
    y, par = dp // 2, dp % 2
    other = 1 - par
    partner = (y * 2 + other, me)
    up = (((y + 1) % RING) * 2 + par, me)
    down = (((y + RING - 1) % RING) * 2 + par, me)

    reads = [
        pltpu.make_async_copy(src, dst, in_sem.at[i])
        for i, (src, dst) in enumerate((
            (counts_hbm, counts), (selected_hbm, selected), (old_hbm, old_place),
            (new_hbm, new_place), (acts_hbm, acts), (grads_hbm, grads), (tokens_hbm, tokens),
            (master_hbm, master), (first_hbm, first), (second_hbm, second),
        ))
    ]
    for read in reads:
        read.start()

    barrier = pltpu.get_barrier_semaphore()
    for peer in (partner, up, down):
        pl.semaphore_signal(barrier, inc=1, device_id=peer, device_id_type=MESH)

    def greet(j, c):
        pl.semaphore_signal(
            barrier, inc=1, device_id=(dp, (me + j) % HOLD), device_id_type=MESH
        )
        return c

    lax.fori_loop(1, HOLD, greet, 0)

    def push(src, dst, send, recv, to):
        copy = pltpu.make_async_remote_copy(
            src_ref=src, dst_ref=dst, send_sem=send, recv_sem=recv,
            device_id=to, device_id_type=MESH,
        )
        copy.start()

    def got(ref, sem):
        pltpu.make_async_copy(ref, ref, sem).wait()

    for i in (0, 1, 2, 3, 5):
        reads[i].wait()

    def find(i, c):
        return c + jnp.where(old_place[i] == me, selected[i], 0)

    expert_id = lax.fori_loop(0, HOLD, find, jnp.int32(0))
    routed = counts[0, expert_id]
    live = lax.broadcasted_iota(jnp.int32, (TOK, 768), 0) < routed
    value = grads[...]
    g_own[...] = jnp.where(live, value, jnp.zeros_like(value))

    def turned(src, dst):
        for i in range(20):
            tile = src[:, i * 128 : (i + 1) * 128].T
            for m in range(4):
                row = i * 128 + m * 32
                block, at_row = row // ROWS, row % ROWS
                dst[block % 2, block // 2, at_row : at_row + 32, :] = tile[m * 32 : (m + 1) * 32]

    reads[4].wait()
    turned(acts, at)
    pl.semaphore_wait(barrier, 3 + HOLD - 1)

    push(g_own, g_in, x_send.at[8], x_recv.at[8], partner)
    for k in (4, 3, 5, 2, 6, 1, 7, 0):
        t = (y + k) % RING
        push(at.at[other, t], at_in.at[k], x_send.at[k], x_recv.at[k], partner)
    reads[6].wait()
    turned(tokens, nt)

    def place(d, c):
        def look(i, c):
            return c + jnp.where(new_place[i] == d, old_place[i], 0)

        order[d] = lax.fori_loop(0, HOLD, look, jnp.int32(0), unroll=True)
        return c

    lax.fori_loop(0, HOLD, place, 0)

    def contribution(k, h):
        t = (y + k) % RING
        cols = slice(h * WIDE, (h + 1) * WIDE)
        return jnp.dot(at[par, t], g_own[:, cols], preferred_element_type=F32) + jnp.dot(
            at_in[k], g_in[:, cols], preferred_element_type=F32
        )

    got(g_in, x_recv.at[8])
    arrived = set()
    for s in range(4):
        if s == 2:
            push(nt.at[other], nt_in, x_send.at[9], x_recv.at[9], partner)
        for c, (h, way, hops) in enumerate(CHAINS):
            if s >= hops:
                continue
            k = (way * (hops - s)) % RING
            if k not in arrived:
                arrived.add(k)
                got(at_in.at[k], x_recv.at[k])
            own = contribution(k, h)
            if s == 0:
                rs_out[c, s] = own.astype(BF16)
            else:
                term[...] = own
                got(rs_in.at[c, s - 1], rs_recv.at[c, s - 1])
                rs_out[c, s] = (rs_in[c, s - 1].astype(F32) + term[...]).astype(BF16)
            push(
                rs_out.at[c, s], rs_in.at[c, s], rs_send.at[c, s], rs_recv.at[c, s],
                up if way == 1 else down,
            )
    got(at_in.at[0], x_recv.at[0])

    def one_phase_out(stage, relay, send, recv, first_relay):
        for lane in range(4):

            def go(z, c, lane=lane):
                j = 4 * z + lane
                n = j - first_relay

                @pl.when((j != me) & (n >= 0) & (n < RELAYS))
                def _():
                    push(stage.at[n], relay.at[me], send, recv, (dp, j))

                return c

            lax.fori_loop(0, HOLD // 4, go, 0)

    for i in (7, 8, 9):
        reads[i].wait()
    for h in range(2):
        term[...] = contribution(0, h)
        for c, (half, way, hops) in enumerate(CHAINS):
            if half == h:
                got(rs_in.at[c, hops - 1], rs_recv.at[c, hops - 1])
        ends = [(c, hops - 1) for c, (half, _, hops) in enumerate(CHAINS) if half == h]
        for k in range(10):
            for q in range(3):
                rows = slice(16 * k, 16 * k + 16)
                local = slice(128 * q, 128 * q + 128)
                cols = slice(h * WIDE + 128 * q, h * WIDE + 128 * q + 128)
                total = term[rows, local]
                for c, s in ends:
                    total = total + rs_in[c, s, rows, local].astype(F32)
                w, m, v = adamw(master[rows, cols], first[rows, cols], second[rows, cols], total)
                p = 3 * k + q
                stage_w[h, p] = w.astype(BF16)
                stage_m[p, 2 * h] = m.astype(BF16)
                stage_m[p, 2 * h + 1] = v.astype(BF16)
        one_phase_out(stage_w.at[h], relay_w[h], p_send.at[0, h], p_recv.at[0, h], 0)

        @pl.when(me < RELAYS)
        def _():
            relay_w[h][me] = stage_w[h, me]

    def two_phase_out(relay, ordered, final, send, recv, first_relay):
        slot = me - first_relay

        @pl.when((me >= first_relay) & (me < first_relay + RELAYS))
        def _():
            got(relay.at[pl.ds(0, HOLD - 1)], recv[0])

            def go(d, c):
                ordered[d] = relay[order[d]]

                @pl.when(d != me)
                def _():
                    push(ordered.at[d], final.at[slot], send[1], recv[1], (dp, d))

                return c

            lax.fori_loop(0, HOLD, go, 0)
            final[slot] = ordered[me]

    def two_phase_in(final, recv, first_relay):
        relaying = (me >= first_relay) & (me < first_relay + RELAYS)

        @pl.when(relaying)
        def _():
            got(final.at[pl.ds(0, RELAYS - 1)], recv)

        @pl.when(jnp.logical_not(relaying))
        def _():
            got(final, recv)

    for h in range(2):
        two_phase_out(
            relay_w[h], sorted_w.at[h], new_w.at[h],
            (p_send.at[0, h], p_send.at[1, h]), (p_recv.at[0, h], p_recv.at[1, h]), 0,
        )
    for h in range(2):
        two_phase_in(new_w.at[h], p_recv.at[1, h], 0)
        for p in range(RELAYS):
            k, q = p // 3, p % 3
            gathered[h, y, 16 * k : 16 * k + 16, 128 * q : 128 * q + 128] = new_w[h, p]
        for c, (half, way, hops) in enumerate(CHAINS):
            if half == h:
                mine = gathered.at[h, y]
                push(mine, mine, ag_send.at[c, 0], ag_recv.at[c, 0], up if way == 1 else down)
    one_phase_out(stage_m, relay_m, p_send.at[0, 2], p_recv.at[0, 2], 2)

    @pl.when(me >= 2)
    def _():
        relay_m[me] = stage_m[me - 2]

    for p in range(RELAYS):
        k, q = p // 3, p % 3
        for h in range(2):
            cols = slice(h * WIDE + 128 * q, h * WIDE + 128 * q + 128)
            out_w[16 * k : 16 * k + 16, cols] = new_w[h, p].astype(F32)

    got(nt_in, x_recv.at[9])
    for i in range(10):
        ntx[0:128, 128 * i : 128 * i + 128] = jnp.concatenate(
            [nt_in[(128 * i + 32 * m) // ROWS, (128 * i + 32 * m) % ROWS : (128 * i + 32 * m) % ROWS + 32] for m in range(4)], axis=0
        ).T
        ntx[128:256, 128 * i : 128 * i + 128] = jnp.concatenate(
            [nt[par, (128 * i + 32 * m) // ROWS, (128 * i + 32 * m) % ROWS : (128 * i + 32 * m) % ROWS + 32] for m in range(4)], axis=0
        ).T

    def forward_out(h):
        whole = gathered[h].reshape(RING * ROWS, WIDE)
        f_out[h] = jnp.dot(ntx[0:128], whole, preferred_element_type=F32).astype(BF16)
        push(f_out.at[h], f_in.at[h], f_send.at[h], f_recv.at[h], partner)

    for s in range(1, 5):
        for c, (h, way, hops) in enumerate(CHAINS):
            if s > hops:
                continue
            block = gathered.at[h, (y - way * s) % RING]
            got(block, ag_recv.at[c, s - 1])
            if s < hops:
                push(block, block, ag_send.at[c, s], ag_recv.at[c, s], up if way == 1 else down)
            if s == 4:
                forward_out(h)
        if s == 2:
            two_phase_out(
                relay_m, sorted_m, new_m,
                (p_send.at[0, 2], p_send.at[1, 2]), (p_recv.at[0, 2], p_recv.at[1, 2]), 2,
            )
    for h in range(2):
        whole = gathered[h].reshape(RING * ROWS, WIDE)
        f_own[h] = jnp.dot(ntx[128:256], whole, preferred_element_type=F32)

    two_phase_in(new_m, p_recv.at[1, 2], 2)
    for p in range(RELAYS):
        k, q = p // 3, p % 3
        for h in range(2):
            cols = slice(h * WIDE + 128 * q, h * WIDE + 128 * q + 128)
            out_m[16 * k : 16 * k + 16, cols] = new_m[p, 2 * h].astype(F32)
            out_v[16 * k : 16 * k + 16, cols] = new_m[p, 2 * h + 1].astype(F32)

    for h in range(2):
        got(f_in.at[h], f_recv.at[h])
        out_f[:, h * WIDE : (h + 1) * WIDE] = (f_own[h] + f_in[h].astype(F32)).astype(BF16)

    for k in range(8):
        got(at_in.at[0], x_send.at[k])
    got(g_own, x_send.at[8])
    got(nt_in, x_send.at[9])
    for c, (h, way, hops) in enumerate(CHAINS):
        for s in range(hops):
            got(rs_out.at[c, s], rs_send.at[c, s])
            got(gathered.at[0, 0], ag_send.at[c, s])
    for h in range(2):
        got(f_out.at[h], f_send.at[h])

    def sent(stage, relay, one, two, first_relay):
        relaying = (me >= first_relay) & (me < first_relay + RELAYS)

        @pl.when(relaying)
        def _():
            got(stage.at[pl.ds(0, RELAYS - 1)], one)
            got(relay.at[pl.ds(0, HOLD - 1)], two)

        @pl.when(jnp.logical_not(relaying))
        def _():
            got(stage, one)

    for h in range(2):
        sent(stage_w.at[h], relay_w[h], p_send.at[0, h], p_send.at[1, h], 0)
    sent(stage_m, relay_m, p_send.at[0, 2], p_send.at[1, 2], 2)


def write(w, m, v, f, out_w, out_m, out_v, out_f, w_held, m_held, v_held, f_held, sems):
    held = (w_held, m_held, v_held, f_held)
    reads = [
        pltpu.make_async_copy(src, dst, sems.at[0, i])
        for i, (src, dst) in enumerate(zip((w, m, v, f), held))
    ]
    writes = [
        pltpu.make_async_copy(src, dst, sems.at[1, i])
        for i, (src, dst) in enumerate(zip(held, (out_w, out_m, out_v, out_f)))
    ]
    for copy in reads:
        copy.start()
    for copy, after in zip(reads, writes):
        copy.wait()
        after.start()
    for copy in writes:
        copy.wait()


def body(
    acts, out_grads, next_tokens, master, first_moment, second_moment,
    counts, selected, old_place, new_place,
):
    vmem = pl.BlockSpec(memory_space=pltpu.VMEM)
    anywhere = pl.BlockSpec(memory_space=pl.ANY)
    state = jax.ShapeDtypeStruct((ROWS, 768), F32)
    w, m, v, f = pl.pallas_call(
        kernel,
        out_shape=(state, state, state, jax.ShapeDtypeStruct((TOK, 768), BF16)),
        in_specs=[anywhere] * 10,
        out_specs=(vmem,) * 4,
        scratch_shapes=[
            pltpu.SMEM(counts.shape, jnp.int32),
            pltpu.SMEM((HOLD,), jnp.int32),
            pltpu.SMEM((HOLD,), jnp.int32),
            pltpu.SMEM((HOLD,), jnp.int32),
            pltpu.VMEM((TOK, 2560), BF16),
            pltpu.VMEM((TOK, 768), BF16),
            pltpu.VMEM((TOK, 2560), BF16),
            pltpu.VMEM((ROWS, 768), F32),
            pltpu.VMEM((ROWS, 768), F32),
            pltpu.VMEM((ROWS, 768), F32),
            pltpu.SemaphoreType.DMA((10,)),
            pltpu.SMEM((HOLD,), jnp.int32),
            pltpu.VMEM((2, RING, ROWS, TOK), BF16),
            pltpu.VMEM((2, RING, ROWS, TOK), BF16),
            pltpu.VMEM((RING, ROWS, TOK), BF16),
            pltpu.VMEM((RING, ROWS, TOK), BF16),
            pltpu.VMEM((2 * TOK, RING * ROWS), BF16),
            pltpu.VMEM((TOK, 768), BF16),
            pltpu.VMEM((TOK, 768), BF16),
            pltpu.VMEM((ROWS, WIDE), F32),
            pltpu.VMEM((4, 4, ROWS, WIDE), BF16),
            pltpu.VMEM((4, 4, ROWS, WIDE), BF16),
            pltpu.VMEM((2, RELAYS, 16, 128), BF16),
            pltpu.VMEM((HOLD, 16, 128), BF16),
            pltpu.VMEM((HOLD, 16, 128), BF16),
            pltpu.VMEM((2, HOLD, 16, 128), BF16),
            pltpu.VMEM((RELAYS, 4, 16, 128), BF16),
            pltpu.VMEM((HOLD, 4, 16, 128), BF16),
            pltpu.VMEM((HOLD, 4, 16, 128), BF16),
            pltpu.VMEM((2, RELAYS, 16, 128), BF16),
            pltpu.VMEM((RELAYS, 4, 16, 128), BF16),
            pltpu.VMEM((2, RING, ROWS, WIDE), BF16),
            pltpu.VMEM((2, TOK, WIDE), BF16),
            pltpu.VMEM((2, TOK, WIDE), BF16),
            pltpu.VMEM((2, TOK, WIDE), F32),
            pltpu.SemaphoreType.DMA((10,)),
            pltpu.SemaphoreType.DMA((10,)),
            pltpu.SemaphoreType.DMA((4, 4)),
            pltpu.SemaphoreType.DMA((4, 4)),
            pltpu.SemaphoreType.DMA((4, 4)),
            pltpu.SemaphoreType.DMA((4, 4)),
            pltpu.SemaphoreType.DMA((2, 3)),
            pltpu.SemaphoreType.DMA((2, 3)),
            pltpu.SemaphoreType.DMA((2,)),
            pltpu.SemaphoreType.DMA((2,)),
        ],
        compiler_params=pltpu.CompilerParams(
            collective_id=0, has_side_effects=True, vmem_limit_bytes=60 * 2**20
        ),
    )(
        counts, selected, old_place, new_place,
        acts[0], out_grads[0], next_tokens[0], master[0], first_moment[0], second_moment[0],
    )
    w, m, v, f = pl.pallas_call(
        write,
        out_shape=(state, state, state, jax.ShapeDtypeStruct((TOK, 768), BF16)),
        in_specs=[anywhere] * 4,
        out_specs=(anywhere,) * 4,
        scratch_shapes=[pltpu.VMEM((ROWS, 768), F32)] * 3
        + [pltpu.VMEM((TOK, 768), BF16), pltpu.SemaphoreType.DMA((2, 4))],
        compiler_params=pltpu.CompilerParams(vmem_limit_bytes=60 * 2**20),
    )(w, m, v, f)
    return w[None], m[None], v[None], f[None]


def solution(mesh):
    both = P("expert", "dp", None)
    return jax.shard_map(
        body,
        mesh=mesh,
        in_specs=(both,) * 6 + (P("dp", None), P(), P(), P()),
        out_specs=(both,) * 4,
        check_vma=False,
    )
```

```python
import jax
import jax.numpy as jnp
from jax import lax
from jax.experimental import pallas as pl
from jax.experimental.pallas import tpu as pltpu
from jax.sharding import PartitionSpec as P

MESH = pl.DeviceIdType.MESH

beta_first = 0.9
beta_second = 0.95
bias_first = 1.0 - 0.9**10
bias_second = 1.0 - 0.95**10
learn_rate = 0.01
decay_rate = 0.1
epsilon = 1e-08

RING = 8
ROWS = 160
WIDE = 384
TOK = 128
HOLD = 32
RELAYS = 30
F32 = jnp.float32
BF16 = jnp.bfloat16
CHAINS = ((0, 1, 4), (1, -1, 4), (1, 1, 3), (0, -1, 3))


def adamw(weights, moment_one, moment_two, gradient):
    moment_one = beta_first * moment_one + (1.0 - beta_first) * gradient
    moment_two = beta_second * moment_two + (1.0 - beta_second) * gradient * gradient
    update = (
        moment_one / bias_first / (jnp.sqrt(moment_two / bias_second) + epsilon)
        + decay_rate * weights
    )
    return (weights - learn_rate * update, moment_one, moment_two)


def kernel(
    counts_hbm, selected_hbm, old_hbm, new_hbm,
    acts_hbm, grads_hbm, tokens_hbm, master_hbm, first_hbm, second_hbm,
    out_w, out_m, out_v, out_f,
    counts, selected, old_place, new_place, acts, grads, tokens, master, first, second, in_sem,
    order, at, nt, at_in, nt_in, ntx, g_own, g_in, term,
    rs_out, rs_in, stage_w, relay_a, relay_b, sorted_w, stage_m, relay_m, sorted_m, new_w, new_m,
    gathered, f_out, f_in, f_own,
    x_send, x_recv, rs_send, rs_recv, ag_send, ag_recv, p_send, p_recv, f_send, f_recv,
):
    dp, me = lax.axis_index("dp"), lax.axis_index("expert")
    relay_w = (relay_a, relay_b)
    y, par = dp // 2, dp % 2
    other = 1 - par
    partner = (y * 2 + other, me)
    up = (((y + 1) % RING) * 2 + par, me)
    down = (((y + RING - 1) % RING) * 2 + par, me)

    reads = [
        pltpu.make_async_copy(src, dst, in_sem.at[i])
        for i, (src, dst) in enumerate((
            (counts_hbm, counts), (selected_hbm, selected), (old_hbm, old_place),
            (new_hbm, new_place), (acts_hbm, acts), (grads_hbm, grads), (tokens_hbm, tokens),
            (master_hbm, master), (first_hbm, first), (second_hbm, second),
        ))
    ]
    for read in reads:
        read.start()

    barrier = pltpu.get_barrier_semaphore()
    for peer in (partner, up, down):
        pl.semaphore_signal(barrier, inc=1, device_id=peer, device_id_type=MESH)

    def greet(j, c):
        pl.semaphore_signal(
            barrier, inc=1, device_id=(dp, (me + j) % HOLD), device_id_type=MESH
        )
        return c

    lax.fori_loop(1, HOLD, greet, 0)

    def push(src, dst, send, recv, to):
        copy = pltpu.make_async_remote_copy(
            src_ref=src, dst_ref=dst, send_sem=send, recv_sem=recv,
            device_id=to, device_id_type=MESH,
        )
        copy.start()

    def got(ref, sem):
        pltpu.make_async_copy(ref, ref, sem).wait()

    for i in (0, 1, 2, 3, 5):
        reads[i].wait()

    def find(i, c):
        return c + jnp.where(old_place[i] == me, selected[i], 0)

    expert_id = lax.fori_loop(0, HOLD, find, jnp.int32(0))
    routed = counts[0, expert_id]
    live = lax.broadcasted_iota(jnp.int32, (TOK, 768), 0) < routed
    value = grads[...]
    g_own[...] = jnp.where(live, value, jnp.zeros_like(value))

    def turned(src, dst):
        for i in range(20):
            tile = src[:, i * 128 : (i + 1) * 128].T
            for m in range(4):
                row = i * 128 + m * 32
                block, at_row = row // ROWS, row % ROWS
                dst[block % 2, block // 2, at_row : at_row + 32, :] = tile[m * 32 : (m + 1) * 32]

    reads[4].wait()
    turned(acts, at)
    pl.semaphore_wait(barrier, 3 + HOLD - 1)

    push(g_own, g_in, x_send.at[8], x_recv.at[8], partner)
    for k in (4, 3, 5, 2, 6, 1, 7, 0):
        t = (y + k) % RING
        push(at.at[other, t], at_in.at[k], x_send.at[k], x_recv.at[k], partner)
    reads[6].wait()
    turned(tokens, nt)

    def place(d, c):
        def look(i, c):
            return c + jnp.where(new_place[i] == d, old_place[i], 0)

        order[d] = lax.fori_loop(0, HOLD, look, jnp.int32(0), unroll=True)
        return c

    lax.fori_loop(0, HOLD, place, 0)

    def contribution(k, h):
        t = (y + k) % RING
        cols = slice(h * WIDE, (h + 1) * WIDE)
        return jnp.dot(at[par, t], g_own[:, cols], preferred_element_type=F32) + jnp.dot(
            at_in[k], g_in[:, cols], preferred_element_type=F32
        )

    got(g_in, x_recv.at[8])
    arrived = set()
    for s in range(4):
        if s == 2:
            push(nt.at[other], nt_in, x_send.at[9], x_recv.at[9], partner)
        for c, (h, way, hops) in enumerate(CHAINS):
            if s >= hops:
                continue
            k = (way * (hops - s)) % RING
            if k not in arrived:
                arrived.add(k)
                got(at_in.at[k], x_recv.at[k])
            own = contribution(k, h)
            if s == 0:
                rs_out[c, s] = own.astype(BF16)
            else:
                term[...] = own
                got(rs_in.at[c, s - 1], rs_recv.at[c, s - 1])
                rs_out[c, s] = (rs_in[c, s - 1].astype(F32) + term[...]).astype(BF16)
            push(
                rs_out.at[c, s], rs_in.at[c, s], rs_send.at[c, s], rs_recv.at[c, s],
                up if way == 1 else down,
            )
    got(at_in.at[0], x_recv.at[0])

    def one_phase_out(stage, relay, send, recv, first_relay):
        for lane in range(4):

            def go(z, c, lane=lane):
                j = 4 * z + lane
                n = j - first_relay

                @pl.when((j != me) & (n >= 0) & (n < RELAYS))
                def _():
                    push(stage.at[n], relay.at[me], send, recv, (dp, j))

                return c

            lax.fori_loop(0, HOLD // 4, go, 0)

    for i in (7, 8, 9):
        reads[i].wait()
    for h in range(2):
        term[...] = contribution(0, h)
        for c, (half, way, hops) in enumerate(CHAINS):
            if half == h:
                got(rs_in.at[c, hops - 1], rs_recv.at[c, hops - 1])
        ends = [(c, hops - 1) for c, (half, _, hops) in enumerate(CHAINS) if half == h]
        for k in range(10):
            for q in range(3):
                rows = slice(16 * k, 16 * k + 16)
                local = slice(128 * q, 128 * q + 128)
                cols = slice(h * WIDE + 128 * q, h * WIDE + 128 * q + 128)
                total = term[rows, local]
                for c, s in ends:
                    total = total + rs_in[c, s, rows, local].astype(F32)
                w, m, v = adamw(master[rows, cols], first[rows, cols], second[rows, cols], total)
                p = 3 * k + q
                stage_w[h, p] = w.astype(BF16)
                stage_m[p, 2 * h] = m.astype(BF16)
                stage_m[p, 2 * h + 1] = v.astype(BF16)
        one_phase_out(stage_w.at[h], relay_w[h], p_send.at[0, h], p_recv.at[0, h], 0)

        @pl.when(me < RELAYS)
        def _():
            relay_w[h][me] = stage_w[h, me]

    def two_phase_out(relay, ordered, final, send, recv, first_relay):
        slot = me - first_relay

        @pl.when((me >= first_relay) & (me < first_relay + RELAYS))
        def _():
            got(relay.at[pl.ds(0, HOLD - 1)], recv[0])

            def go(d, c):
                ordered[d] = relay[order[d]]

                @pl.when(d != me)
                def _():
                    push(ordered.at[d], final.at[slot], send[1], recv[1], (dp, d))

                return c

            lax.fori_loop(0, HOLD, go, 0)
            final[slot] = ordered[me]

    def two_phase_in(final, recv, first_relay):
        relaying = (me >= first_relay) & (me < first_relay + RELAYS)

        @pl.when(relaying)
        def _():
            got(final.at[pl.ds(0, RELAYS - 1)], recv)

        @pl.when(jnp.logical_not(relaying))
        def _():
            got(final, recv)

    for h in range(2):
        two_phase_out(
            relay_w[h], sorted_w.at[h], new_w.at[h],
            (p_send.at[0, h], p_send.at[1, h]), (p_recv.at[0, h], p_recv.at[1, h]), 0,
        )
    for h in range(2):
        two_phase_in(new_w.at[h], p_recv.at[1, h], 0)
        for p in range(RELAYS):
            k, q = p // 3, p % 3
            gathered[h, y, 16 * k : 16 * k + 16, 128 * q : 128 * q + 128] = new_w[h, p]
        for c, (half, way, hops) in enumerate(CHAINS):
            if half == h:
                mine = gathered.at[h, y]
                push(mine, mine, ag_send.at[c, 0], ag_recv.at[c, 0], up if way == 1 else down)
    one_phase_out(stage_m, relay_m, p_send.at[0, 2], p_recv.at[0, 2], 2)

    @pl.when(me >= 2)
    def _():
        relay_m[me] = stage_m[me - 2]

    got(nt_in, x_recv.at[9])
    for i in range(10):
        ntx[0:128, 128 * i : 128 * i + 128] = jnp.concatenate(
            [nt_in[(128 * i + 32 * m) // ROWS, (128 * i + 32 * m) % ROWS : (128 * i + 32 * m) % ROWS + 32] for m in range(4)], axis=0
        ).T
        ntx[128:256, 128 * i : 128 * i + 128] = jnp.concatenate(
            [nt[par, (128 * i + 32 * m) // ROWS, (128 * i + 32 * m) % ROWS : (128 * i + 32 * m) % ROWS + 32] for m in range(4)], axis=0
        ).T

    def forward_out(h):
        whole = gathered[h].reshape(RING * ROWS, WIDE)
        f_out[h] = jnp.dot(ntx[0:128], whole, preferred_element_type=F32).astype(BF16)
        push(f_out.at[h], f_in.at[h], f_send.at[h], f_recv.at[h], partner)

    for s in range(1, 5):
        for c, (h, way, hops) in enumerate(CHAINS):
            if s > hops:
                continue
            block = gathered.at[h, (y - way * s) % RING]
            got(block, ag_recv.at[c, s - 1])
            if s < hops:
                push(block, block, ag_send.at[c, s], ag_recv.at[c, s], up if way == 1 else down)
            if s == 4:
                forward_out(h)
        if s == 2:
            two_phase_out(
                relay_m, sorted_m, new_m,
                (p_send.at[0, 2], p_send.at[1, 2]), (p_recv.at[0, 2], p_recv.at[1, 2]), 2,
            )
    for h in range(2):
        whole = gathered[h].reshape(RING * ROWS, WIDE)
        f_own[h] = jnp.dot(ntx[128:256], whole, preferred_element_type=F32)

    for p in range(RELAYS):
        k, q = p // 3, p % 3
        for h in range(2):
            cols = slice(h * WIDE + 128 * q, h * WIDE + 128 * q + 128)
            out_w[16 * k : 16 * k + 16, cols] = new_w[h, p].astype(F32)

    two_phase_in(new_m, p_recv.at[1, 2], 2)
    for p in range(RELAYS):
        k, q = p // 3, p % 3
        for h in range(2):
            cols = slice(h * WIDE + 128 * q, h * WIDE + 128 * q + 128)
            out_m[16 * k : 16 * k + 16, cols] = new_m[p, 2 * h].astype(F32)
            out_v[16 * k : 16 * k + 16, cols] = new_m[p, 2 * h + 1].astype(F32)

    for h in range(2):
        got(f_in.at[h], f_recv.at[h])
        out_f[:, h * WIDE : (h + 1) * WIDE] = (f_own[h] + f_in[h].astype(F32)).astype(BF16)

    for k in range(8):
        got(at_in.at[0], x_send.at[k])
    got(g_own, x_send.at[8])
    got(nt_in, x_send.at[9])
    for c, (h, way, hops) in enumerate(CHAINS):
        for s in range(hops):
            got(rs_out.at[c, s], rs_send.at[c, s])
            got(gathered.at[0, 0], ag_send.at[c, s])
    for h in range(2):
        got(f_out.at[h], f_send.at[h])

    def sent(stage, relay, one, two, first_relay):
        relaying = (me >= first_relay) & (me < first_relay + RELAYS)

        @pl.when(relaying)
        def _():
            got(stage.at[pl.ds(0, RELAYS - 1)], one)
            got(relay.at[pl.ds(0, HOLD - 1)], two)

        @pl.when(jnp.logical_not(relaying))
        def _():
            got(stage, one)

    for h in range(2):
        sent(stage_w.at[h], relay_w[h], p_send.at[0, h], p_send.at[1, h], 0)
    sent(stage_m, relay_m, p_send.at[0, 2], p_send.at[1, 2], 2)


def write(w, m, v, f, out_w, out_m, out_v, out_f, w_held, m_held, v_held, f_held, sems):
    held = (w_held, m_held, v_held, f_held)
    reads = [
        pltpu.make_async_copy(src, dst, sems.at[0, i])
        for i, (src, dst) in enumerate(zip((w, m, v, f), held))
    ]
    writes = [
        pltpu.make_async_copy(src, dst, sems.at[1, i])
        for i, (src, dst) in enumerate(zip(held, (out_w, out_m, out_v, out_f)))
    ]
    for copy in reads:
        copy.start()
    for copy, after in zip(reads, writes):
        copy.wait()
        after.start()
    for copy in writes:
        copy.wait()


def body(
    acts, out_grads, next_tokens, master, first_moment, second_moment,
    counts, selected, old_place, new_place,
):
    vmem = pl.BlockSpec(memory_space=pltpu.VMEM)
    anywhere = pl.BlockSpec(memory_space=pl.ANY)
    state = jax.ShapeDtypeStruct((ROWS, 768), F32)
    w, m, v, f = pl.pallas_call(
        kernel,
        out_shape=(state, state, state, jax.ShapeDtypeStruct((TOK, 768), BF16)),
        in_specs=[anywhere] * 10,
        out_specs=(vmem,) * 4,
        scratch_shapes=[
            pltpu.SMEM(counts.shape, jnp.int32),
            pltpu.SMEM((HOLD,), jnp.int32),
            pltpu.SMEM((HOLD,), jnp.int32),
            pltpu.SMEM((HOLD,), jnp.int32),
            pltpu.VMEM((TOK, 2560), BF16),
            pltpu.VMEM((TOK, 768), BF16),
            pltpu.VMEM((TOK, 2560), BF16),
            pltpu.VMEM((ROWS, 768), F32),
            pltpu.VMEM((ROWS, 768), F32),
            pltpu.VMEM((ROWS, 768), F32),
            pltpu.SemaphoreType.DMA((10,)),
            pltpu.SMEM((HOLD,), jnp.int32),
            pltpu.VMEM((2, RING, ROWS, TOK), BF16),
            pltpu.VMEM((2, RING, ROWS, TOK), BF16),
            pltpu.VMEM((RING, ROWS, TOK), BF16),
            pltpu.VMEM((RING, ROWS, TOK), BF16),
            pltpu.VMEM((2 * TOK, RING * ROWS), BF16),
            pltpu.VMEM((TOK, 768), BF16),
            pltpu.VMEM((TOK, 768), BF16),
            pltpu.VMEM((ROWS, WIDE), F32),
            pltpu.VMEM((4, 4, ROWS, WIDE), BF16),
            pltpu.VMEM((4, 4, ROWS, WIDE), BF16),
            pltpu.VMEM((2, RELAYS, 16, 128), BF16),
            pltpu.VMEM((HOLD, 16, 128), BF16),
            pltpu.VMEM((HOLD, 16, 128), BF16),
            pltpu.VMEM((2, HOLD, 16, 128), BF16),
            pltpu.VMEM((RELAYS, 4, 16, 128), BF16),
            pltpu.VMEM((HOLD, 4, 16, 128), BF16),
            pltpu.VMEM((HOLD, 4, 16, 128), BF16),
            pltpu.VMEM((2, RELAYS, 16, 128), BF16),
            pltpu.VMEM((RELAYS, 4, 16, 128), BF16),
            pltpu.VMEM((2, RING, ROWS, WIDE), BF16),
            pltpu.VMEM((2, TOK, WIDE), BF16),
            pltpu.VMEM((2, TOK, WIDE), BF16),
            pltpu.VMEM((2, TOK, WIDE), F32),
            pltpu.SemaphoreType.DMA((10,)),
            pltpu.SemaphoreType.DMA((10,)),
            pltpu.SemaphoreType.DMA((4, 4)),
            pltpu.SemaphoreType.DMA((4, 4)),
            pltpu.SemaphoreType.DMA((4, 4)),
            pltpu.SemaphoreType.DMA((4, 4)),
            pltpu.SemaphoreType.DMA((2, 3)),
            pltpu.SemaphoreType.DMA((2, 3)),
            pltpu.SemaphoreType.DMA((2,)),
            pltpu.SemaphoreType.DMA((2,)),
        ],
        compiler_params=pltpu.CompilerParams(
            collective_id=0, has_side_effects=True, vmem_limit_bytes=60 * 2**20
        ),
    )(
        counts, selected, old_place, new_place,
        acts[0], out_grads[0], next_tokens[0], master[0], first_moment[0], second_moment[0],
    )
    w, m, v, f = pl.pallas_call(
        write,
        out_shape=(state, state, state, jax.ShapeDtypeStruct((TOK, 768), BF16)),
        in_specs=[anywhere] * 4,
        out_specs=(anywhere,) * 4,
        scratch_shapes=[pltpu.VMEM((ROWS, 768), F32)] * 3
        + [pltpu.VMEM((TOK, 768), BF16), pltpu.SemaphoreType.DMA((2, 4))],
        compiler_params=pltpu.CompilerParams(vmem_limit_bytes=60 * 2**20),
    )(w, m, v, f)
    return w[None], m[None], v[None], f[None]


def solution(mesh):
    both = P("expert", "dp", None)
    return jax.shard_map(
        body,
        mesh=mesh,
        in_specs=(both,) * 6 + (P("dp", None), P(), P(), P()),
        out_specs=(both,) * 4,
        check_vma=False,
    )
```
